32 devices in a mesh: groups: 2 (over x), tiles: 16 (over z, y, core).
Axes of the slice: x: 2, y: 2, z: 4, core: 2. Of those that a mesh axis runs over, the one named last changes fastest.
Arguments:
- video_q: bfloat16 [8192, 3072], P(('groups', 'tiles')), parts along dimension 0, may hold values from -88 to 88, as said below
- video_k: bfloat16 [8192, 3072], P(('groups', 'tiles')), parts along dimension 0, may hold values from -4 to 4, as said below
- video_v: bfloat16 [8192, 3072], P(('groups', 'tiles')), parts along dimension 0, may hold values from -5 to 5
- text_q: bfloat16 [512, 3072], P('groups'), parts along dimension 0, may hold values from -88 to 88
- text_k: bfloat16 [512, 3072], P('groups'), parts along dimension 0, may hold values from -5 to 5
- text_v: bfloat16 [512, 3072], P('groups'), parts along dimension 0, may hold values from -5 to 5
- window: int32 [32, 6], P('tiles'), may hold values from 0 to 13, as said below
- counts: int32 [64], P(('groups', 'tiles')), parts along dimension 0, may hold values from 1 to 128, as said below
- text_count: int32 [2], P('groups'), parts along dimension 0, may hold values from 64 to 256
Outputs:
- video_out: bfloat16 [8192, 3072], P(('groups', 'tiles')), parts along dimension 0
- text_out: bfloat16 [512, 3072], P(('groups', 'tiles')), parts along dimension 0
The draws below stay inside these ranges and needn't reach their ends.
There are 2 independent parts, one for each index of `groups`. The reference program is written for one: setup_inputs(seed, part) draws one part's arguments, and reference() takes and returns one part's arrays. A program takes and returns all parts, laid end to end along the dimension named above; an argument that names none is the same for every part. Nothing has to cross between parts.
Inputs may be any that keep to these rules, and one draw needn't show every extreme that they name: `video_q`: queries drawn for the problem. `video_k`: keys drawn for the problem. `window`: each row names 6 different codes, among them always 3, 6, 9 and 12. `counts`: valid tokens are the first slots of a tile.
All inputs are finite; a program needn't handle non-finite values.
Results may differ from the reference program's by a relative error of at most 0.003.
Values may be sent and summed in bfloat16 or wider, within the bound.
A program may use at most 192 MiB of HBM per device.

```python
import math
import jax
import jax.numpy as jnp
from jax import lax

HEADS = 24
HD = 128
D = 3072
TOK = 128
CT = 2
NR = 4
WIN = 6
TEXT = 256
TILES_ALL = 32
VIDEO = 4096
N_TILES = 16


def base_keys(key):
    keys_drawn = jnp.clip(jax.random.normal(jax.random.fold_in(key, 11), (VIDEO, D), jnp.float32), -4.0, 4.0)
    return keys_drawn


def draw_video_k(key, part):
    return base_keys(key).astype(jnp.bfloat16)


def draw_video_q(key, part):
    drawn = 2.5 * jnp.clip(jax.random.normal(jax.random.fold_in(key, 23), (VIDEO, D), jnp.float32), -4.0, 4.0)
    return drawn.astype(jnp.bfloat16)


def draw_text_q(key, part):
    drawn = 3.5 * jnp.clip(jax.random.normal(jax.random.fold_in(key, 37), (TEXT, D), jnp.float32), -4.0, 4.0)
    return drawn.astype(jnp.bfloat16)


def draw_window(key, part):
    fixed_codes = jnp.broadcast_to(jnp.array([3, 6, 9, 12], jnp.int32), (TILES_ALL, 4))
    other_codes = jnp.array([0, 1, 2, 4, 5, 7, 8, 10, 11, 13], jnp.int32)
    scores = jax.random.randint(jax.random.fold_in(key, 61), (TILES_ALL, 10), 0, 1 << 20, dtype=jnp.int32)
    scores = scores * 16 + jnp.arange(10, dtype=jnp.int32)[None, :]
    _, picked = lax_top(-scores)
    extra = other_codes[picked]
    return jnp.concatenate([fixed_codes, extra], axis=1)[:, :WIN].astype(jnp.int32)


def lax_top(values):
    return jax.lax.top_k(values, WIN - 4)


def draw_counts(key, part):
    tile_ids = jnp.arange(TILES_ALL, dtype=jnp.int32)
    device = tile_ids // CT
    column = tile_ids % CT
    tiles_devices = TILES_ALL // CT
    row_block = (device + tiles_devices // 2 + NR + NR // 2) % tiles_devices % NR
    edge = (row_block == NR - 1) | (column == CT - 1)
    drawn = jax.random.randint(jax.random.fold_in(key, 5), (TILES_ALL,), 1, TOK + 1, dtype=jnp.int32)
    return jnp.where(edge, drawn, TOK).astype(jnp.int32)


def draw_text_count(key, part):
    drawn = jax.random.randint(jax.random.fold_in(key, 41), (1,), TEXT // 4, TEXT, dtype=jnp.int32)
    return jnp.where(part % 2 == 1, TEXT, drawn).astype(jnp.int32)


def level_of(own_key, dims, pieces, smallest, top_value):
    factor_of = 1.0
    for position, shards_of in pieces:
        heights = jax.random.uniform(jax.random.fold_in(jax.random.fold_in(own_key, 6), position), (shards_of,), jnp.float32, smallest / len(pieces), top_value / len(pieces))
        factor_of = factor_of * jnp.repeat(jnp.exp(heights), dims[position] // shards_of).reshape((-1,) + (1,) * (len(dims) - 1 - position))
    return factor_of


def normal_values(rng, extent, scale, limit, split=(), kind=jnp.bfloat16):
    values = scale * jax.random.normal(rng, extent, jnp.float32)
    if split:
        values = values * level_of(rng, extent, split, -0.22, 0.18)
    return jnp.clip(values, -limit, limit).astype(kind)


def setup_inputs(seed: int = 0, part: int = 0) -> dict:
    key_of = jax.random.split(jax.random.key(seed), 10)
    part_splits = jax.random.split(jax.random.fold_in(key_of[9], part), 10)
    video_q = draw_video_q(jax.random.fold_in(jax.random.fold_in(key_of[9], part), 71), part)
    video_k = draw_video_k(jax.random.fold_in(jax.random.fold_in(key_of[9], part), 71), part)
    video_v = normal_values(part_splits[2], (VIDEO, D), 1.0, 5.0, ((0, 16),))
    text_q = draw_text_q(jax.random.fold_in(jax.random.fold_in(key_of[9], part), 71), part)
    text_k = normal_values(part_splits[4], (TEXT, D), 1.0, 5.0)
    text_v = normal_values(part_splits[5], (TEXT, D), 1.0, 5.0)
    window = draw_window(jax.random.fold_in(key_of[9], 71), part)
    counts = draw_counts(jax.random.fold_in(jax.random.fold_in(key_of[9], part), 71), part)
    text_count = draw_text_count(jax.random.fold_in(jax.random.fold_in(key_of[9], part), 71), part)
    return dict(video_q=video_q, video_k=video_k, video_v=video_v, text_q=text_q, text_k=text_k, text_v=text_v, window=window, counts=counts, text_count=text_count)


def reference(video_q, video_k, video_v, text_q, text_k, text_v, window, counts, text_count):
    score_scale = 1.0 / math.sqrt(HD)
    devices_all = N_TILES
    blocks_time = devices_all // NR
    layout_shift = devices_all // 2 + NR + NR // 2
    spread = ((1, 1), (1, 1), (1, 1), (0, 0), (0, 0), (0, 0))
    key_rolled = jnp.roll(video_k.reshape(devices_all, CT, TOK, HEADS, HD), layout_shift, axis=0)
    value_rolled = jnp.roll(video_v.reshape(devices_all, CT, TOK, HEADS, HD), layout_shift, axis=0)
    count_rolled = jnp.roll(counts.reshape(devices_all, CT), layout_shift, axis=0)
    key_grid = jnp.pad(key_rolled.reshape(blocks_time, NR, CT, TOK, HEADS, HD), spread)
    value_grid = jnp.pad(value_rolled.reshape(blocks_time, NR, CT, TOK, HEADS, HD), spread)
    count_grid = jnp.pad(count_rolled.reshape(blocks_time, NR, CT), ((1, 1), (1, 1), (1, 1)))
    query_tiles = video_q.reshape(devices_all, CT, TOK, HEADS, HD)
    window_rows = window.reshape(devices_all, CT, WIN)
    count_rows = counts.reshape(devices_all, CT)
    text_valid = jnp.arange(TEXT, dtype=jnp.int32) < text_count[0]
    time_step = jnp.array([0, -1, 1, 0, 0], jnp.int32)
    row_step = jnp.array([0, 0, 0, -1, 1], jnp.int32)
    text_keys = text_k.reshape(TEXT, HEADS, HD).astype(jnp.float32)
    text_values = text_v.reshape(TEXT, HEADS, HD).astype(jnp.float32)
    slot_ids = jnp.arange(TOK, dtype=jnp.int32)

    def one_device(device):
        spot = ((device + layout_shift) % devices_all).astype(jnp.int32)
        tblock = (spot // NR).astype(jnp.int32)
        rblock = (spot % NR).astype(jnp.int32)
        zero_at = jnp.zeros((), jnp.int32)
        key_near = lax.dynamic_slice(key_grid, (tblock, rblock, zero_at, zero_at, zero_at, zero_at), (3, 3, CT + 2, TOK, HEADS, HD))
        value_near = lax.dynamic_slice(value_grid, (tblock, rblock, zero_at, zero_at, zero_at, zero_at), (3, 3, CT + 2, TOK, HEADS, HD))
        count_near = lax.dynamic_slice(count_grid, (tblock, rblock, zero_at), (3, 3, CT + 2))
        window_codes = window_rows[device]
        cell_codes = jnp.concatenate([jnp.ones((CT, 1), jnp.int32), (window_codes + (window_codes >= 1)).astype(jnp.int32)], axis=1)
        block_of = cell_codes // 3
        column_at = jnp.arange(CT, dtype=jnp.int32)[:, None] + cell_codes % 3
        time_at = 1 + time_step[block_of]
        row_at = 1 + row_step[block_of]
        keys_chosen = key_near[time_at, row_at, column_at].reshape(CT, (WIN + 1) * TOK, HEADS, HD).astype(jnp.float32)
        values_chosen = value_near[time_at, row_at, column_at].reshape(CT, (WIN + 1) * TOK, HEADS, HD).astype(jnp.float32)
        counts_chosen = count_near[time_at, row_at, column_at]
        key_valid = (slot_ids[None, None, :] < counts_chosen[:, :, None]).reshape(CT, (WIN + 1) * TOK)
        queries = query_tiles[device].astype(jnp.float32)
        video_scores = jnp.einsum('cqhd,ckhd->chqk', queries, keys_chosen) * score_scale
        video_scores = jnp.where(key_valid[:, None, None, :], video_scores, -jnp.inf)
        text_scores = jnp.einsum('cqhd,khd->chqk', queries, text_keys) * score_scale
        text_scores = jnp.where(text_valid[None, None, None, :], text_scores, -jnp.inf)
        row_top = jnp.maximum(lax.optimization_barrier(jnp.max(video_scores, axis=-1)), lax.optimization_barrier(jnp.max(text_scores, axis=-1)))[..., None]
        video_probs = jnp.exp(video_scores - row_top)
        text_probs = jnp.exp(text_scores - row_top)
        denom = lax.optimization_barrier(jnp.sum(video_probs, axis=-1)) + lax.optimization_barrier(jnp.sum(text_probs, axis=-1))
        video_round = lax.optimization_barrier(video_probs.astype(jnp.bfloat16)).astype(jnp.float32)
        text_round = lax.optimization_barrier(text_probs.astype(jnp.bfloat16)).astype(jnp.float32)
        numer = jnp.einsum('chqk,ckhd->cqhd', video_round, values_chosen) + jnp.einsum('chqk,khd->cqhd', text_round, text_values)
        result = numer / jnp.transpose(denom, (0, 2, 1))[..., None]
        query_valid = slot_ids[None, :] < count_rows[device][:, None]
        return jnp.where(query_valid[:, :, None, None], result, 0.0).astype(jnp.bfloat16)
    device_ids = jnp.arange(devices_all, dtype=jnp.int32)
    video_out = lax.map(one_device, device_ids).reshape(VIDEO, D)
    key_blocks = video_k.reshape(devices_all, CT * TOK, HEADS, HD)
    value_blocks = video_v.reshape(devices_all, CT * TOK, HEADS, HD)
    valid_blocks = (slot_ids[None, None, :] < count_rows[:, :, None]).reshape(devices_all, CT * TOK)
    text_queries = text_q.reshape(TEXT, HEADS, HD).astype(jnp.float32)

    def block_scores(device):
        scores = jnp.einsum('qhd,khd->hqk', text_queries, key_blocks[device].astype(jnp.float32)) * score_scale
        return jnp.where(valid_blocks[device][None, None, :], scores, -jnp.inf)

    def block_top(device):
        return lax.optimization_barrier(jnp.max(block_scores(device), axis=-1))
    global_top = lax.optimization_barrier(jnp.max(lax.map(block_top, device_ids), axis=0))

    def accumulate(carry, device):
        weights = jnp.exp(block_scores(device) - global_top[..., None])
        denom_part = lax.optimization_barrier(jnp.sum(weights, axis=-1))
        weights_round = lax.optimization_barrier(weights.astype(jnp.bfloat16)).astype(jnp.float32)
        numer_part = jnp.einsum('hqk,khd->qhd', weights_round, value_blocks[device].astype(jnp.float32))
        return ((carry[0] + numer_part, carry[1] + denom_part.T), None)
    start_sums = (jnp.zeros((TEXT, HEADS, HD), jnp.float32), jnp.zeros((TEXT, HEADS), jnp.float32))
    (numer_all, denom_all), _ = lax.scan(accumulate, start_sums, device_ids)
    text_result = numer_all / denom_all[..., None]
    text_out = jnp.where(text_valid[:, None, None], text_result, 0.0).astype(jnp.bfloat16).reshape(TEXT, D)
    return (video_out, text_out)
```

```python
import functools
import math

import jax
import jax.numpy as jnp
from jax import lax
from jax.experimental import pallas as pl
from jax.experimental.pallas import tpu as pltpu
from jax.sharding import PartitionSpec as P

HEADS = 24
HD = 128
NR = 4
WIDTH = 256
LOG2E_SCALE = math.log2(math.e) / math.sqrt(HD)
MESH = pl.DeviceIdType.MESH
NT = (((1,), (1,)), ((), ()))


def text_kernel(q_ref, k_ref, v_ref, bias_ref, num_ref, stat_ref):
    step = pl.program_id(0)

    @pl.when(step == 0)
    def _():
        stat_ref[...] = jnp.zeros_like(stat_ref)

    lanes = lax.broadcasted_iota(jnp.int32, stat_ref.shape, 1)
    bias = bias_ref[0:1, :]
    for h in range(WIDTH // HD):
        cols = slice(h * HD, (h + 1) * HD)
        s = lax.dot_general(
            q_ref[:, cols], k_ref[:, cols], NT, preferred_element_type=jnp.float32
        )
        s = s + bias
        top = jnp.max(s, axis=1, keepdims=True)
        p = jnp.exp2((s - top) * LOG2E_SCALE)
        total = jnp.sum(p, axis=1, keepdims=True)
        num = jnp.dot(p.astype(jnp.bfloat16), v_ref[:, cols], preferred_element_type=jnp.float32)
        num_ref[:, cols] = num.astype(jnp.bfloat16)
        head = step * (WIDTH // HD) + h
        stat = jnp.where(lanes == head, top, stat_ref[...])
        stat_ref[...] = jnp.where(lanes == head + 32, total, stat)


def main_kernel(
    n, q_ref, k_ref, v_ref, tk_ref, tv_ref, pick_ref, own_ref, qv_ref, tnum_ref, tstat_ref,
    out_ref, rnum_ref, rstat_ref,
    near, near_bias, send_sem, recv_sem, bsend_sem, brecv_sem, tsend_sem, trecv_sem, own_sem,
):
    group = lax.axis_index("groups")
    me = lax.axis_index("tiles")
    spot = lax.rem(me + n // 2 + NR + NR // 2, n)
    row = lax.rem(spot, NR)
    time = lax.div(spot, NR)
    chunks = q_ref.shape[1] // WIDTH
    has = (time > 0, time < n // NR - 1, row > 0, row < NR - 1)
    sends = (has[1], has[0], has[3], has[2])
    offs = (-NR, NR, -1, 1)
    targets = tuple((group, lax.rem(me - o + n, n)) for o in offs)

    barrier = pltpu.get_barrier_semaphore()

    def greet(i, _):
        pl.semaphore_signal(
            barrier, inc=1, device_id=(group, lax.rem(me + i, n)), device_id_type=MESH
        )
        return 0

    lax.fori_loop(1, n, greet, 0)
    pl.semaphore_wait(barrier, n - 1)

    def bias_copy(d):
        return pltpu.make_async_remote_copy(
            src_ref=own_ref, dst_ref=near_bias.at[d], send_sem=bsend_sem.at[d],
            recv_sem=brecv_sem.at[d], device_id=targets[d], device_id_type=MESH,
        )

    def block_copy(d, kv, c):
        cols = pl.ds(pl.multiple_of(c * WIDTH, WIDTH), WIDTH)
        return pltpu.make_async_remote_copy(
            src_ref=(k_ref, v_ref)[kv].at[:, cols], dst_ref=near.at[d, kv, c],
            send_sem=send_sem.at[d, kv, c], recv_sem=recv_sem.at[d, kv, c],
            device_id=targets[d], device_id_type=MESH,
        )

    def text_copies(i):
        to = lax.rem(me + i, n)
        return (
            pltpu.make_async_remote_copy(
                src_ref=tnum_ref.at[to], dst_ref=rnum_ref.at[me], send_sem=tsend_sem.at[0, i],
                recv_sem=trecv_sem.at[0, i], device_id=(group, to), device_id_type=MESH,
            ),
            pltpu.make_async_remote_copy(
                src_ref=tstat_ref.at[to], dst_ref=rstat_ref.at[me], send_sem=tsend_sem.at[1, i],
                recv_sem=trecv_sem.at[1, i], device_id=(group, to), device_id_type=MESH,
            ),
        )

    def text_arrivals(i):
        origin = lax.rem(me - i + n, n)
        return (
            pltpu.make_async_remote_copy(
                src_ref=tnum_ref.at[origin], dst_ref=rnum_ref.at[origin],
                send_sem=tsend_sem.at[0, i], recv_sem=trecv_sem.at[0, i],
                device_id=(group, origin), device_id_type=MESH,
            ),
            pltpu.make_async_remote_copy(
                src_ref=tstat_ref.at[origin], dst_ref=rstat_ref.at[origin],
                send_sem=tsend_sem.at[1, i], recv_sem=trecv_sem.at[1, i],
                device_id=(group, origin), device_id_type=MESH,
            ),
        )

    for d in range(4):
        @pl.when(sends[d])
        def _(d=d):
            bias_copy(d).start()

    def start_chunk(c, _):
        for d in range(4):
            @pl.when(sends[d])
            def _(d=d):
                block_copy(d, 0, c).start()
                block_copy(d, 1, c).start()
        return 0

    lax.fori_loop(0, chunks, start_chunk, 0)

    def start_text(i, _):
        for copy in text_copies(i):
            copy.start()
        return 0

    lax.fori_loop(1, n, start_text, 0)
    own_num = pltpu.make_async_copy(tnum_ref.at[me], rnum_ref.at[me], own_sem.at[0])
    own_stat = pltpu.make_async_copy(tstat_ref.at[me], rstat_ref.at[me], own_sem.at[1])
    own_num.start()
    own_stat.start()

    for d in range(4):
        @pl.when(jnp.logical_not(has[d]))
        def _(d=d):
            near_bias[d] = jnp.full(near_bias.shape[1:], -jnp.inf, jnp.float32)

            def clear(c, _):
                near[d, 0, c] = jnp.zeros(near.shape[3:], jnp.bfloat16)
                near[d, 1, c] = jnp.zeros(near.shape[3:], jnp.bfloat16)
                return 0

            lax.fori_loop(0, chunks, clear, 0)

        @pl.when(has[d])
        def _(d=d):
            bias_copy(d).wait_recv()

    tokens = q_ref.shape[0]
    half = tokens // 2

    def attend(c, _):
        for d in range(4):
            @pl.when(has[d])
            def _(d=d):
                block_copy(d, 0, c).wait_recv()
                block_copy(d, 1, c).wait_recv()
        for h in range(WIDTH // HD):
            cols = pl.ds(pl.multiple_of(c * WIDTH + h * HD, HD), HD)
            here = slice(h * HD, (h + 1) * HD)
            q = q_ref[:, cols]
            scores = []
            for b in range(6):
                if b == 0:
                    key, extra = k_ref[:, cols], own_ref[0:1, :]
                elif b == 5:
                    key, extra = tk_ref[:, cols], None
                else:
                    key, extra = near[b - 1, 0, c, :, here], near_bias[b - 1, 0:1, :]
                s = lax.dot_general(q, key, NT, preferred_element_type=jnp.float32)
                parts = []
                for t in range(2):
                    bias = pick_ref[b, t:t + 1, :]
                    if extra is not None:
                        bias = bias + extra
                    parts.append(s[t * half:(t + 1) * half] + bias)
                scores.append(jnp.concatenate(parts, axis=0))
            top = functools.reduce(jnp.maximum, scores)
            top = jnp.max(top, axis=1, keepdims=True)
            total, num = None, None
            for b in range(6):
                p = jnp.exp2((scores[b] - top) * LOG2E_SCALE)
                total = p if total is None else total + p
                if b == 0:
                    value = v_ref[:, cols]
                elif b == 5:
                    value = tv_ref[:, cols]
                else:
                    value = near[b - 1, 1, c, :, here]
                term = jnp.dot(p.astype(jnp.bfloat16), value, preferred_element_type=jnp.float32)
                num = term if num is None else num + term
            total = jnp.sum(total, axis=1, keepdims=True)
            result = jnp.where(qv_ref[...] > 0, num / total, 0.0)
            out_ref[:, cols] = result.astype(jnp.bfloat16)
        return 0

    lax.fori_loop(0, chunks, attend, 0)

    for d in range(4):
        @pl.when(sends[d])
        def _(d=d):
            bias_copy(d).wait_send()

    def finish_chunk(c, _):
        for d in range(4):
            @pl.when(sends[d])
            def _(d=d):
                block_copy(d, 0, c).wait_send()
                block_copy(d, 1, c).wait_send()
        return 0

    lax.fori_loop(0, chunks, finish_chunk, 0)

    def finish_text(i, _):
        for copy in text_arrivals(i):
            copy.wait_recv()
        for copy in text_copies(i):
            copy.wait_send()
        return 0

    lax.fori_loop(1, n, finish_text, 0)
    own_num.wait()
    own_stat.wait()


def per_device(video_q, video_k, video_v, text_q, text_k, text_v, window, counts, text_count):
    n = lax.axis_size("tiles")
    position = lax.axis_index("tiles")
    tiles = counts.shape[0]
    tokens, width = video_q.shape
    tok = tokens // tiles
    text = text_q.shape[0]
    share = text // n
    slots = jnp.arange(tok, dtype=jnp.int32)
    valid = (slots[None, :] < counts[:, None]).reshape(-1)
    own_bias = jnp.broadcast_to(jnp.where(valid, 0.0, -jnp.inf)[None, :], (8, tokens))
    codes = jnp.concatenate([jnp.ones((tiles, 1), jnp.int32), window + (window >= 1)], axis=1)
    column = jnp.arange(tiles, dtype=jnp.int32)[:, None] + codes % 3 - 1
    block_ids = jnp.arange(5, dtype=jnp.int32)[:, None, None, None]
    column_ids = jnp.arange(tiles, dtype=jnp.int32)[None, None, :, None]
    hit = jnp.any(
        (codes[None, :, None, :] // 3 == block_ids) & (column[None, :, None, :] == column_ids),
        axis=-1,
    )
    pick = jnp.broadcast_to(hit[..., None], (5, tiles, tiles, tok)).reshape(5, tiles, tokens)
    text_ok = jnp.arange(text, dtype=jnp.int32) < text_count[0]
    text_pick = jnp.broadcast_to(text_ok[None, None, :], (1, tiles, text))
    pick = jnp.where(jnp.concatenate([pick, text_pick], axis=0), 0.0, -jnp.inf)
    pick = jnp.pad(pick, ((0, 0), (0, 8 - tiles), (0, 0)))
    query_valid = valid.astype(jnp.float32)[:, None]

    step_in = pl.BlockSpec((tokens, WIDTH), lambda i: (0, i))
    text_step = pl.BlockSpec((text, WIDTH), lambda i: (0, i))
    tnum, tstat = pl.pallas_call(
        text_kernel,
        grid=(width // WIDTH,),
        out_shape=(
            jax.ShapeDtypeStruct((text, width), jnp.bfloat16),
            jax.ShapeDtypeStruct((text, 128), jnp.float32),
        ),
        in_specs=[text_step, step_in, step_in, pl.BlockSpec((8, tokens), lambda i: (0, 0))],
        out_specs=(text_step, pl.BlockSpec((text, 128), lambda i: (0, 0))),
    )(text_q, video_k, video_v, own_bias)

    vmem = pl.BlockSpec(memory_space=pltpu.VMEM)
    hbm = pl.BlockSpec(memory_space=pl.ANY)
    chunks = width // WIDTH
    dma = pltpu.SemaphoreType.DMA
    video_out, rnum, rstat = pl.pallas_call(
        functools.partial(main_kernel, n),
        out_shape=(
            jax.ShapeDtypeStruct((tokens, width), jnp.bfloat16),
            jax.ShapeDtypeStruct((n, share, width), jnp.bfloat16),
            jax.ShapeDtypeStruct((n, share, 128), jnp.float32),
        ),
        in_specs=[vmem] * 8 + [hbm, hbm],
        out_specs=(vmem, hbm, hbm),
        scratch_shapes=[
            pltpu.VMEM((4, 2, chunks, tokens, WIDTH), jnp.bfloat16),
            pltpu.VMEM((4, 8, tokens), jnp.float32),
            dma((4, 2, chunks)),
            dma((4, 2, chunks)),
            dma((4,)),
            dma((4,)),
            dma((2, n)),
            dma((2, n)),
            dma((2,)),
        ],
        compiler_params=pltpu.CompilerParams(
            collective_id=0, has_side_effects=True, vmem_limit_bytes=48 * 1024 * 1024
        ),
    )(
        video_q, video_k, video_v, text_k, text_v, pick, own_bias, query_valid,
        tnum.reshape(n, share, width), tstat.reshape(n, share, 128),
    )

    tops, sums = rstat[..., :HEADS], rstat[..., 32:32 + HEADS]
    scale = jnp.exp2((tops - jnp.max(tops, axis=0)) * LOG2E_SCALE)
    den = jnp.sum(sums * scale, axis=0)
    parts = rnum.reshape(n, share, HEADS, HD).astype(jnp.float32)
    text_result = jnp.sum(parts * scale[..., None], axis=0) / den[..., None]
    row_ids = position * share + jnp.arange(share, dtype=jnp.int32)
    text_out = jnp.where((row_ids < text_count[0])[:, None, None], text_result, 0.0)
    return (video_out, text_out.astype(jnp.bfloat16).reshape(share, width))


def solution(mesh):
    return jax.shard_map(
        per_device,
        mesh=mesh,
        in_specs=(
            P(("groups", "tiles"), None),
            P(("groups", "tiles"), None),
            P(("groups", "tiles"), None),
            P("groups", None),
            P("groups", None),
            P("groups", None),
            P("tiles", None),
            P(("groups", "tiles")),
            P("groups"),
        ),
        out_specs=(P(("groups", "tiles"), None), P(("groups", "tiles"), None)),
        check_vma=False,
    )
```

```python
import functools
import math

import jax
import jax.numpy as jnp
from jax import lax
from jax.experimental import pallas as pl
from jax.experimental.pallas import tpu as pltpu
from jax.sharding import PartitionSpec as P

HEADS = 24
HD = 128
NR = 4
WIDTH = 256
LOG2E_SCALE = math.log2(math.e) / math.sqrt(HD)
MESH = pl.DeviceIdType.MESH
NT = (((1,), (1,)), ((), ()))


def main_kernel(
    n, q_ref, k_ref, v_ref, tq_ref, tk_ref, tv_ref, pick_ref, own_ref, qv_ref, tok_ref,
    out_ref, tout_ref,
    near, near_bias, relay, tnum, tstat, rnum, rstat,
    send_sem, recv_sem, bsend_sem, brecv_sem, fsend_sem, rsend_sem, rrecv_sem, tsend_sem, trecv_sem,
):
    group = lax.axis_index("groups")
    me = lax.axis_index("tiles")
    last = n // NR - 1
    chunks = q_ref.shape[1] // WIDTH
    per_chunk = WIDTH // HD
    tokens = q_ref.shape[0]
    half = tokens // 2
    share = tout_ref.shape[0]

    def at(offset):
        return lax.rem(me + offset + n, n)

    def time_of(index):
        return lax.div(lax.rem(index + n // 2 + NR + NR // 2, n), NR)

    row = lax.rem(me + n // 2 + NR + NR // 2, NR)
    time = time_of(me)
    side = lax.rem(me, 2)
    has = (time > 0, time < last, row > 0, row < NR - 1)
    offs = (-NR, NR, -1, 1)
    even = lax.rem(row, 2) == 0
    odd = lax.rem(row, 2) == 1
    quarter = lax.rem(me, 4)
    wrap_up = (quarter == 1) & (me < NR) & (time > 0)
    wrap_down = (quarter == 1) & (me >= n - NR) & (time < last)
    relay_up = (quarter == 3) & (me < NR) & (time_of(at(-2)) > 0)
    relay_down = (quarter == 3) & (me >= n - NR) & (time_of(at(-2)) < last)
    forward_down = (row == 1) & (time > 0)
    forward_up = (row == 2) & (time < last)

    barrier = pltpu.get_barrier_semaphore()

    def greet(i, _):
        pl.semaphore_signal(barrier, inc=1, device_id=(group, at(i)), device_id_type=MESH)
        return 0

    lax.fori_loop(1, n, greet, 0)
    pl.semaphore_wait(barrier, n - 1)

    def remote(source, target, sent, got, to):
        return pltpu.make_async_remote_copy(
            src_ref=source, dst_ref=target, send_sem=sent, recv_sem=got,
            device_id=(group, to), device_id_type=MESH,
        )

    def block(kv, c):
        cols = pl.ds(pl.multiple_of(c * WIDTH, WIDTH), WIDTH)
        return (k_ref, v_ref)[kv].at[:, cols]

    def bias_copy(d):
        return remote(own_ref, near_bias.at[d], bsend_sem.at[d], brecv_sem.at[d], at(-offs[d]))

    def direct(d, kv, c):
        return remote(
            block(kv, c), near.at[d, kv, c], send_sem.at[d, kv, c], recv_sem.at[d, kv, c], at(-offs[d])
        )

    def to_relay(d, kv, c):
        return remote(
            block(kv, c), relay.at[kv, c], send_sem.at[d, kv, c], rrecv_sem.at[kv, c], at(2)
        )

    def from_relay(d, kv, c):
        return remote(
            relay.at[kv, c], near.at[d, kv, c], rsend_sem.at[kv, c], recv_sem.at[d, kv, c],
            at(-2 - offs[d]),
        )

    def forward(d, kv, c):
        slot, to = (2, at(1 - NR)) if d == 0 else (3, at(NR - 1))
        return remote(
            near.at[d, kv, c], near.at[slot, kv, c], fsend_sem.at[kv, c], recv_sem.at[slot, kv, c], to
        )

    pair_sends = (((2, even), (0, 1)), ((3, odd), (0, 1)))
    far_sends = (
        ((0, (time < last) & jnp.logical_not(wrap_down)), (0, 1)),
        ((0, wrap_down), (1,)),
        ((1, (time > 0) & jnp.logical_not(wrap_up)), (0, 1)),
        ((2, (row == 1) & (time == last)), (0, 1)),
        ((3, (row == 2) & (time == 0)), (0, 1)),
    )
    relay_sends = (((0, wrap_down), (0,)), ((1, wrap_up), (0, 1)))
    onward = (((0, relay_down), (0,)), ((1, relay_up), (0, 1)))
    forwards = (((0, forward_down), (0, 1)), ((1, forward_up), (0, 1)))

    def each(table, make, act, c):
        for (d, when), kinds in table:
            @pl.when(when)
            def _(d=d, kinds=kinds):
                for kv in kinds:
                    act(make(d, kv, c))

    def start(copy):
        copy.start()

    def wait_send(copy):
        copy.wait_send()

    bias_sends = (has[1], has[0], has[3], has[2])
    for d in range(4):
        @pl.when(bias_sends[d])
        def _(d=d):
            bias_copy(d).start()

    def start_far(c, _):
        each(relay_sends, to_relay, start, c)
        each(far_sends, direct, start, c)

        def pass_on(d, kinds):
            for kv in kinds:
                pltpu.make_async_remote_copy(
                    src_ref=block(kv, c), dst_ref=relay.at[kv, c], send_sem=send_sem.at[d, kv, c],
                    recv_sem=rrecv_sem.at[kv, c], device_id=(group, at(2)), device_id_type=MESH,
                ).wait_recv()
                from_relay(d, kv, c).start()

        for (d, when), kinds in onward:
            @pl.when(when)
            def _(d=d, kinds=kinds):
                pass_on(d, kinds)
        return 0

    def start_pair(c, _):
        each(pair_sends, direct, start, c)
        return 0

    def missing(d):
        near_bias[d] = jnp.full(near_bias.shape[1:], -jnp.inf, jnp.float32)

        def clear(c, _):
            near[d, 0, c] = jnp.zeros(near.shape[3:], jnp.bfloat16)
            near[d, 1, c] = jnp.zeros(near.shape[3:], jnp.bfloat16)
            return 0

        lax.fori_loop(0, chunks, clear, 0)

    lax.fori_loop(0, 2, start_far, 0)
    lax.fori_loop(0, chunks, start_pair, 0)
    for d in range(4):
        @pl.when(jnp.logical_not(has[d]))
        def _(d=d):
            missing(d)

        @pl.when(has[d])
        def _(d=d):
            bias_copy(d).wait_recv()

    text_chunks = chunks // 2
    first = side * text_chunks
    lanes = lax.broadcasted_iota(jnp.int32, (share, 128), 1)

    def pair_arrived(c, _):
        for d, when in ((3, even), (2, odd)):
            @pl.when(when)
            def _(d=d):
                direct(d, 0, c).wait_recv()
                direct(d, 1, c).wait_recv()
        return 0

    lax.fori_loop(0, chunks, pair_arrived, 0)
    pair_slot = 3 - lax.rem(row, 2)
    tstat[...] = jnp.zeros_like(tstat)

    def text_part(j, _):
        c = first + j
        for h in range(per_chunk):
            cols = pl.ds(pl.multiple_of(c * WIDTH + h * HD, HD), HD)
            here = slice(h * HD, (h + 1) * HD)
            to = pl.ds(pl.multiple_of(j * WIDTH + h * HD, HD), HD)
            q = tq_ref[:, cols]
            s0 = lax.dot_general(q, k_ref[:, cols], NT, preferred_element_type=jnp.float32)
            s1 = lax.dot_general(
                q, near[pair_slot, 0, c, :, here], NT, preferred_element_type=jnp.float32
            )
            s0 = s0 + own_ref[0:1, :]
            s1 = s1 + near_bias[pair_slot, 0:1, :]
            top = jnp.max(jnp.maximum(s0, s1), axis=1, keepdims=True)
            p0 = jnp.exp2((s0 - top) * LOG2E_SCALE)
            p1 = jnp.exp2((s1 - top) * LOG2E_SCALE)
            total = jnp.sum(p0 + p1, axis=1, keepdims=True)
            num = None
            for p, value in ((p0, v_ref[:, cols]), (p1, near[pair_slot, 1, c, :, here])):
                high = p.astype(jnp.bfloat16)
                low = (p - high.astype(jnp.float32)).astype(jnp.bfloat16)
                for part in (high, low):
                    term = jnp.dot(part, value, preferred_element_type=jnp.float32)
                    num = term if num is None else num + term
            num = num.astype(jnp.bfloat16)
            head = j * per_chunk + h
            for b in range(n):
                rows = slice(b * share, (b + 1) * share)
                tnum[b, :, to] = num[rows]
                tstat[b, 0] = jnp.where(lanes == head, top[rows], tstat[b, 0])
                tstat[b, 1] = jnp.where(lanes == head, total[rows], tstat[b, 1])
        return 0

    lax.fori_loop(0, text_chunks, text_part, 0)

    def text_copies(i, there, here):
        return (
            remote(tnum.at[there], rnum.at[here], tsend_sem.at[0, i], trecv_sem.at[0, i], there),
            remote(tstat.at[there], rstat.at[here], tsend_sem.at[1, i], trecv_sem.at[1, i], there),
        )

    def start_text(i, _):
        for copy in text_copies(i, at(i), me):
            copy.start()
        return 0

    lax.fori_loop(1, n, start_text, 0)
    rnum[me] = tnum[me]
    rstat[me] = tstat[me]
    lax.fori_loop(2, chunks, start_far, 0)

    waits = (
        (0, has[0]), (1, has[1]),
        (2, has[2] & even), (3, has[3] & odd),
    )

    def attend(c, _):
        for d, when in waits[:2]:
            @pl.when(when)
            def _(d=d):
                direct(d, 0, c).wait_recv()
                direct(d, 1, c).wait_recv()
        each(forwards, forward, start, c)
        for d, when in waits[2:]:
            @pl.when(when)
            def _(d=d):
                direct(d, 0, c).wait_recv()
                direct(d, 1, c).wait_recv()
        for h in range(WIDTH // HD):
            cols = pl.ds(pl.multiple_of(c * WIDTH + h * HD, HD), HD)
            here = slice(h * HD, (h + 1) * HD)
            q = q_ref[:, cols]
            scores = []
            for b in range(6):
                if b == 0:
                    key, extra = k_ref[:, cols], own_ref[0:1, :]
                elif b == 5:
                    key, extra = tk_ref[:, cols], None
                else:
                    key, extra = near[b - 1, 0, c, :, here], near_bias[b - 1, 0:1, :]
                s = lax.dot_general(q, key, NT, preferred_element_type=jnp.float32)
                parts = []
                for t in range(2):
                    bias = pick_ref[b, t:t + 1, :]
                    if extra is not None:
                        bias = bias + extra
                    parts.append(s[t * half:(t + 1) * half] + bias)
                scores.append(jnp.concatenate(parts, axis=0))
            top = functools.reduce(jnp.maximum, scores)
            top = jnp.max(top, axis=1, keepdims=True)
            total, num = None, None
            for b in range(6):
                p = jnp.exp2((scores[b] - top) * LOG2E_SCALE)
                total = p if total is None else total + p
                if b == 0:
                    value = v_ref[:, cols]
                elif b == 5:
                    value = tv_ref[:, cols]
                else:
                    value = near[b - 1, 1, c, :, here]
                term = jnp.dot(p.astype(jnp.bfloat16), value, preferred_element_type=jnp.float32)
                num = term if num is None else num + term
            total = jnp.sum(total, axis=1, keepdims=True)
            result = jnp.where(qv_ref[...] > 0, num / total, 0.0)
            out_ref[:, cols] = result.astype(jnp.bfloat16)
        return 0

    lax.fori_loop(0, chunks, attend, 0)

    def finish(c, _):
        each(pair_sends, direct, wait_send, c)
        each(far_sends, direct, wait_send, c)
        each(relay_sends, to_relay, wait_send, c)
        each(onward, from_relay, wait_send, c)
        each(forwards, forward, wait_send, c)
        return 0

    def text_arrived(i, _):
        for copy in text_copies(i, at(n - i), at(n - i)):
            copy.wait_recv()
        for copy in text_copies(i, at(i), me):
            copy.wait_send()
        return 0

    lax.fori_loop(1, n, text_arrived, 0)

    heads = tnum.shape[2] // HD
    for e in range(2):
        top = lax.fori_loop(
            1, n // 2, lambda i, m: jnp.maximum(m, rstat[2 * i + e, 0]), rstat[e, 0]
        )

        def add(i, carry):
            den, nums = carry
            scale = jnp.exp2((rstat[2 * i + e, 0] - top) * LOG2E_SCALE)
            den = den + scale * rstat[2 * i + e, 1]
            nums = tuple(
                nums[j]
                + rnum[2 * i + e, :, j * HD:(j + 1) * HD].astype(jnp.float32) * scale[:, j:j + 1]
                for j in range(heads)
            )
            return den, nums

        zeros = jnp.zeros((share, HD), jnp.float32)
        den, nums = lax.fori_loop(0, n // 2, add, (zeros, (zeros,) * heads))
        for j in range(heads):
            result = jnp.where(tok_ref[...] > 0, nums[j] / den[:, j:j + 1], 0.0)
            at_head = (e * heads + j) * HD
            tout_ref[:, at_head:at_head + HD] = result.astype(jnp.bfloat16)

    for d in range(4):
        @pl.when(bias_sends[d])
        def _(d=d):
            bias_copy(d).wait_send()
    lax.fori_loop(0, chunks, finish, 0)


def per_device(video_q, video_k, video_v, text_q, text_k, text_v, window, counts, text_count):
    n = lax.axis_size("tiles")
    position = lax.axis_index("tiles")
    tiles = counts.shape[0]
    tokens, width = video_q.shape
    tok = tokens // tiles
    text = text_q.shape[0]
    share = text // n
    slots = jnp.arange(tok, dtype=jnp.int32)
    valid = (slots[None, :] < counts[:, None]).reshape(-1)
    own_bias = jnp.broadcast_to(jnp.where(valid, 0.0, -jnp.inf)[None, :], (8, tokens))
    codes = jnp.concatenate([jnp.ones((tiles, 1), jnp.int32), window + (window >= 1)], axis=1)
    column = jnp.arange(tiles, dtype=jnp.int32)[:, None] + codes % 3 - 1
    block_ids = jnp.arange(5, dtype=jnp.int32)[:, None, None, None]
    column_ids = jnp.arange(tiles, dtype=jnp.int32)[None, None, :, None]
    hit = jnp.any(
        (codes[None, :, None, :] // 3 == block_ids) & (column[None, :, None, :] == column_ids),
        axis=-1,
    )
    pick = jnp.broadcast_to(hit[..., None], (5, tiles, tiles, tok)).reshape(5, tiles, tokens)
    text_ok = jnp.arange(text, dtype=jnp.int32) < text_count[0]
    text_pick = jnp.broadcast_to(text_ok[None, None, :], (1, tiles, text))
    pick = jnp.where(jnp.concatenate([pick, text_pick], axis=0), 0.0, -jnp.inf)
    pick = jnp.pad(pick, ((0, 0), (0, 8 - tiles), (0, 0)))
    query_valid = valid.astype(jnp.float32)[:, None]

    row_ids = position * share + jnp.arange(share, dtype=jnp.int32)
    row_valid = (row_ids < text_count[0]).astype(jnp.float32)[:, None]
    vmem = pl.BlockSpec(memory_space=pltpu.VMEM)
    chunks = width // WIDTH
    dma = pltpu.SemaphoreType.DMA
    video_out, text_out = pl.pallas_call(
        functools.partial(main_kernel, n),
        out_shape=(
            jax.ShapeDtypeStruct((tokens, width), jnp.bfloat16),
            jax.ShapeDtypeStruct((share, width), jnp.bfloat16),
        ),
        in_specs=[vmem] * 10,
        out_specs=(vmem, vmem),
        scratch_shapes=[
            pltpu.VMEM((4, 2, chunks, tokens, WIDTH), jnp.bfloat16),
            pltpu.VMEM((4, 8, tokens), jnp.float32),
            pltpu.VMEM((2, chunks, tokens, WIDTH), jnp.bfloat16),
            pltpu.VMEM((n, share, width // 2), jnp.bfloat16),
            pltpu.VMEM((n, 2, share, 128), jnp.float32),
            pltpu.VMEM((n, share, width // 2), jnp.bfloat16),
            pltpu.VMEM((n, 2, share, 128), jnp.float32),
            dma((4, 2, chunks)),
            dma((4, 2, chunks)),
            dma((4,)),
            dma((4,)),
            dma((2, chunks)),
            dma((2, chunks)),
            dma((2, chunks)),
            dma((2, n)),
            dma((2, n)),
        ],
        compiler_params=pltpu.CompilerParams(
            collective_id=0, has_side_effects=True, vmem_limit_bytes=56 * 1024 * 1024
        ),
    )(
        video_q, video_k, video_v, text_q, text_k, text_v, pick, own_bias, query_valid, row_valid
    )
    return (video_out, text_out)


def solution(mesh):
    return jax.shard_map(
        per_device,
        mesh=mesh,
        in_specs=(
            P(("groups", "tiles"), None),
            P(("groups", "tiles"), None),
            P(("groups", "tiles"), None),
            P("groups", None),
            P("groups", None),
            P("groups", None),
            P("tiles", None),
            P(("groups", "tiles")),
            P("groups"),
        ),
        out_specs=(P(("groups", "tiles"), None), P(("groups", "tiles"), None)),
        check_vma=False,
    )
```

```python
import functools
import math

import jax
import jax.numpy as jnp
from jax import lax
from jax.experimental import pallas as pl
from jax.experimental.pallas import tpu as pltpu
from jax.sharding import PartitionSpec as P

HEADS = 24
HD = 128
NR = 4
WIDTH = 256
LOG2E_SCALE = math.log2(math.e) / math.sqrt(HD)
MESH = pl.DeviceIdType.MESH
NT = (((1,), (1,)), ((), ()))


def main_kernel(
    n, q_ref, k_ref, v_ref, tq_ref, tk_ref, tv_ref, pick_ref, own_ref, qv_ref, tok_ref,
    out_ref, tout_ref,
    near, near_bias, relay, tnum, tstat, rnum, rstat,
    send_sem, recv_sem, bsend_sem, brecv_sem, fsend_sem, rsend_sem, rrecv_sem, tsend_sem, trecv_sem,
):
    group = lax.axis_index("groups")
    me = lax.axis_index("tiles")
    last = n // NR - 1
    chunks = q_ref.shape[1] // WIDTH
    per_chunk = WIDTH // HD
    tokens = q_ref.shape[0]
    half = tokens // 2
    share = tout_ref.shape[0]

    def at(offset):
        return lax.rem(me + offset + n, n)

    def time_of(index):
        return lax.div(lax.rem(index + n // 2 + NR + NR // 2, n), NR)

    row = lax.rem(me + n // 2 + NR + NR // 2, NR)
    time = time_of(me)
    side = lax.rem(me, 2)
    has = (time > 0, time < last, row > 0, row < NR - 1)
    offs = (-NR, NR, -1, 1)
    even = lax.rem(row, 2) == 0
    odd = lax.rem(row, 2) == 1
    quarter = lax.rem(me, 4)
    wrap_up = (quarter == 1) & (me < NR) & (time > 0)
    wrap_down = (quarter == 1) & (me >= n - NR) & (time < last)
    relay_up = (quarter == 3) & (me < NR) & (time_of(at(-2)) > 0)
    relay_down = (quarter == 3) & (me >= n - NR) & (time_of(at(-2)) < last)
    forward_down = (row == 1) & (time > 0)
    forward_up = (row == 2) & (time < last)

    barrier = pltpu.get_barrier_semaphore()

    def greet(i, _):
        pl.semaphore_signal(barrier, inc=1, device_id=(group, at(i)), device_id_type=MESH)
        return 0

    lax.fori_loop(1, n, greet, 0)
    pl.semaphore_wait(barrier, n - 1)

    def remote(source, target, sent, got, to):
        return pltpu.make_async_remote_copy(
            src_ref=source, dst_ref=target, send_sem=sent, recv_sem=got,
            device_id=(group, to), device_id_type=MESH,
        )

    def block(kv, c):
        cols = pl.ds(pl.multiple_of(c * WIDTH, WIDTH), WIDTH)
        return (k_ref, v_ref)[kv].at[:, cols]

    def bias_copy(d):
        return remote(own_ref, near_bias.at[d], bsend_sem.at[d], brecv_sem.at[d], at(-offs[d]))

    def direct(d, kv, c):
        return remote(
            block(kv, c), near.at[d, kv, c], send_sem.at[d, kv, c], recv_sem.at[d, kv, c], at(-offs[d])
        )

    def to_relay(d, kv, c):
        return remote(
            block(kv, c), relay.at[kv, c], send_sem.at[d, kv, c], rrecv_sem.at[kv, c], at(2)
        )

    def from_relay(d, kv, c):
        return remote(
            relay.at[kv, c], near.at[d, kv, c], rsend_sem.at[kv, c], recv_sem.at[d, kv, c],
            at(-2 - offs[d]),
        )

    def forward(d, kv, c):
        slot, to = (2, at(1 - NR)) if d == 0 else (3, at(NR - 1))
        return remote(
            near.at[d, kv, c], near.at[slot, kv, c], fsend_sem.at[kv, c], recv_sem.at[slot, kv, c], to
        )

    pair_sends = (((2, even), (0, 1)), ((3, odd), (0, 1)))
    far_sends = (
        ((0, (time < last) & jnp.logical_not(wrap_down)), (0, 1)),
        ((0, wrap_down), (1,)),
        ((1, (time > 0) & jnp.logical_not(wrap_up)), (0, 1)),
        ((2, (row == 1) & (time == last)), (0, 1)),
        ((3, (row == 2) & (time == 0)), (0, 1)),
    )
    relay_sends = (((0, wrap_down), (0,)), ((1, wrap_up), (0, 1)))
    onward = (((0, relay_down), (0,)), ((1, relay_up), (0, 1)))
    forwards = (((0, forward_down), (0, 1)), ((1, forward_up), (0, 1)))

    def each(table, make, act, c):
        for (d, when), kinds in table:
            @pl.when(when)
            def _(d=d, kinds=kinds):
                for kv in kinds:
                    act(make(d, kv, c))

    def start(copy):
        copy.start()

    def wait_send(copy):
        copy.wait_send()

    bias_sends = (has[1], has[0], has[3], has[2])
    for d in range(4):
        @pl.when(bias_sends[d])
        def _(d=d):
            bias_copy(d).start()

    def start_far(c, _):
        each(relay_sends, to_relay, start, c)
        each(far_sends, direct, start, c)

        def pass_on(d, kinds):
            for kv in kinds:
                pltpu.make_async_remote_copy(
                    src_ref=block(kv, c), dst_ref=relay.at[kv, c], send_sem=send_sem.at[d, kv, c],
                    recv_sem=rrecv_sem.at[kv, c], device_id=(group, at(2)), device_id_type=MESH,
                ).wait_recv()
                from_relay(d, kv, c).start()

        for (d, when), kinds in onward:
            @pl.when(when)
            def _(d=d, kinds=kinds):
                pass_on(d, kinds)
        return 0

    def start_pair(c, _):
        each(pair_sends, direct, start, c)
        return 0

    def missing(d):
        near_bias[d] = jnp.full(near_bias.shape[1:], -jnp.inf, jnp.float32)

        def clear(c, _):
            near[d, 0, c] = jnp.zeros(near.shape[3:], jnp.bfloat16)
            near[d, 1, c] = jnp.zeros(near.shape[3:], jnp.bfloat16)
            return 0

        lax.fori_loop(0, chunks, clear, 0)

    lax.fori_loop(0, 2, start_far, 0)
    lax.fori_loop(0, chunks, start_pair, 0)
    for d in range(4):
        @pl.when(jnp.logical_not(has[d]))
        def _(d=d):
            missing(d)

        @pl.when(has[d])
        def _(d=d):
            bias_copy(d).wait_recv()

    text_chunks = chunks // 2
    first = side * text_chunks
    lanes = lax.broadcasted_iota(jnp.int32, (share, 128), 1)

    def pair_arrived(c, _):
        for d, when in ((3, even), (2, odd)):
            @pl.when(when)
            def _(d=d):
                direct(d, 0, c).wait_recv()
                direct(d, 1, c).wait_recv()
        return 0

    lax.fori_loop(0, chunks, pair_arrived, 0)
    pair_slot = 3 - lax.rem(row, 2)
    tstat[...] = jnp.zeros_like(tstat)

    def text_part(j, _):
        c = first + j
        for h in range(per_chunk):
            cols = pl.ds(pl.multiple_of(c * WIDTH + h * HD, HD), HD)
            here = slice(h * HD, (h + 1) * HD)
            to = pl.ds(pl.multiple_of(j * WIDTH + h * HD, HD), HD)
            q = tq_ref[:, cols]
            s0 = lax.dot_general(q, k_ref[:, cols], NT, preferred_element_type=jnp.float32)
            s1 = lax.dot_general(
                q, near[pair_slot, 0, c, :, here], NT, preferred_element_type=jnp.float32
            )
            s0 = s0 + own_ref[0:1, :]
            s1 = s1 + near_bias[pair_slot, 0:1, :]
            top = jnp.max(jnp.maximum(s0, s1), axis=1, keepdims=True)
            p0 = jnp.exp2((s0 - top) * LOG2E_SCALE)
            p1 = jnp.exp2((s1 - top) * LOG2E_SCALE)
            total = jnp.sum(p0 + p1, axis=1, keepdims=True)
            num = None
            for p, value in ((p0, v_ref[:, cols]), (p1, near[pair_slot, 1, c, :, here])):
                wide = p * 65537.0
                high = wide - (wide - p)
                for part in (high, p - high):
                    term = jnp.dot(
                        part.astype(jnp.bfloat16), value, preferred_element_type=jnp.float32
                    )
                    num = term if num is None else num + term
            num = num.astype(jnp.bfloat16)
            head = j * per_chunk + h
            for b in range(n):
                rows = slice(b * share, (b + 1) * share)
                tnum[b, :, to] = num[rows]
                stat = jnp.where(lanes == head, top[rows], tstat[b])
                tstat[b] = jnp.where(lanes == head + 64, total[rows], stat)
        return 0

    lax.fori_loop(0, text_chunks, text_part, 0)

    def text_copies(i, there, here):
        return (
            remote(tnum.at[there], rnum.at[here], tsend_sem.at[0, i], trecv_sem.at[0, i], there),
            remote(tstat.at[there], rstat.at[here], tsend_sem.at[1, i], trecv_sem.at[1, i], there),
        )

    def start_text(i, _):
        for copy in text_copies(i, at(i), me):
            copy.start()
        return 0

    lax.fori_loop(1, n, start_text, 0)
    rnum[me] = tnum[me]
    rstat[me] = tstat[me]
    lax.fori_loop(2, chunks, start_far, 0)

    waits = (
        (0, has[0]), (1, has[1]),
        (2, has[2] & even), (3, has[3] & odd),
    )

    def attend(c, _):
        for d, when in waits[:2]:
            @pl.when(when)
            def _(d=d):
                direct(d, 0, c).wait_recv()
                direct(d, 1, c).wait_recv()
        each(forwards, forward, start, c)
        for d, when in waits[2:]:
            @pl.when(when)
            def _(d=d):
                direct(d, 0, c).wait_recv()
                direct(d, 1, c).wait_recv()
        for h in range(WIDTH // HD):
            cols = pl.ds(pl.multiple_of(c * WIDTH + h * HD, HD), HD)
            here = slice(h * HD, (h + 1) * HD)
            q = q_ref[:, cols]
            scores = []
            for b in range(6):
                if b == 0:
                    key, extra = k_ref[:, cols], own_ref[0:1, :]
                elif b == 5:
                    key, extra = tk_ref[:, cols], None
                else:
                    key, extra = near[b - 1, 0, c, :, here], near_bias[b - 1, 0:1, :]
                s = lax.dot_general(q, key, NT, preferred_element_type=jnp.float32)
                parts = []
                for t in range(2):
                    bias = pick_ref[b, t:t + 1, :]
                    if extra is not None:
                        bias = bias + extra
                    parts.append(s[t * half:(t + 1) * half] + bias)
                scores.append(jnp.concatenate(parts, axis=0))
            top = functools.reduce(jnp.maximum, scores)
            top = jnp.max(top, axis=1, keepdims=True)
            total, num = None, None
            for b in range(6):
                p = jnp.exp2((scores[b] - top) * LOG2E_SCALE)
                total = p if total is None else total + p
                if b == 0:
                    value = v_ref[:, cols]
                elif b == 5:
                    value = tv_ref[:, cols]
                else:
                    value = near[b - 1, 1, c, :, here]
                term = jnp.dot(p.astype(jnp.bfloat16), value, preferred_element_type=jnp.float32)
                num = term if num is None else num + term
            total = jnp.sum(total, axis=1, keepdims=True)
            result = jnp.where(qv_ref[...] > 0, num / total, 0.0)
            out_ref[:, cols] = result.astype(jnp.bfloat16)
        return 0

    lax.fori_loop(0, chunks, attend, 0)

    def finish(c, _):
        each(pair_sends, direct, wait_send, c)
        each(far_sends, direct, wait_send, c)
        each(relay_sends, to_relay, wait_send, c)
        each(onward, from_relay, wait_send, c)
        each(forwards, forward, wait_send, c)
        return 0

    def text_arrived(i, _):
        for copy in text_copies(i, at(n - i), at(n - i)):
            copy.wait_recv()
        for copy in text_copies(i, at(i), me):
            copy.wait_send()
        return 0

    lax.fori_loop(1, n, text_arrived, 0)

    heads = tnum.shape[2] // HD
    for e in range(2):
        top = lax.fori_loop(
            1, n // 2, lambda i, m: jnp.maximum(m, rstat[2 * i + e]), rstat[e]
        )

        def add(i, carry):
            den, nums = carry
            stat = rstat[2 * i + e]
            scale = jnp.exp2((stat - top) * LOG2E_SCALE)
            den = den + scale * jnp.roll(stat, 64, axis=1)
            nums = tuple(
                nums[j]
                + rnum[2 * i + e, :, j * HD:(j + 1) * HD].astype(jnp.float32) * scale[:, j:j + 1]
                for j in range(heads)
            )
            return den, nums

        zeros = jnp.zeros((share, HD), jnp.float32)
        den, nums = lax.fori_loop(0, n // 2, add, (zeros, (zeros,) * heads))
        for j in range(heads):
            result = jnp.where(tok_ref[...] > 0, nums[j] / den[:, j:j + 1], 0.0)
            at_head = (e * heads + j) * HD
            tout_ref[:, at_head:at_head + HD] = result.astype(jnp.bfloat16)

    for d in range(4):
        @pl.when(bias_sends[d])
        def _(d=d):
            bias_copy(d).wait_send()
    lax.fori_loop(0, chunks, finish, 0)


def per_device(video_q, video_k, video_v, text_q, text_k, text_v, window, counts, text_count):
    n = lax.axis_size("tiles")
    position = lax.axis_index("tiles")
    tiles = counts.shape[0]
    tokens, width = video_q.shape
    tok = tokens // tiles
    text = text_q.shape[0]
    share = text // n
    slots = jnp.arange(tok, dtype=jnp.int32)
    valid = (slots[None, :] < counts[:, None]).reshape(-1)
    own_bias = jnp.broadcast_to(jnp.where(valid, 0.0, -jnp.inf)[None, :], (8, tokens))
    codes = jnp.concatenate([jnp.ones((tiles, 1), jnp.int32), window + (window >= 1)], axis=1)
    column = jnp.arange(tiles, dtype=jnp.int32)[:, None] + codes % 3 - 1
    block_ids = jnp.arange(5, dtype=jnp.int32)[:, None, None, None]
    column_ids = jnp.arange(tiles, dtype=jnp.int32)[None, None, :, None]
    hit = jnp.any(
        (codes[None, :, None, :] // 3 == block_ids) & (column[None, :, None, :] == column_ids),
        axis=-1,
    )
    pick = jnp.broadcast_to(hit[..., None], (5, tiles, tiles, tok)).reshape(5, tiles, tokens)
    text_ok = jnp.arange(text, dtype=jnp.int32) < text_count[0]
    text_pick = jnp.broadcast_to(text_ok[None, None, :], (1, tiles, text))
    pick = jnp.where(jnp.concatenate([pick, text_pick], axis=0), 0.0, -jnp.inf)
    pick = jnp.pad(pick, ((0, 0), (0, 8 - tiles), (0, 0)))
    query_valid = valid.astype(jnp.float32)[:, None]

    row_ids = position * share + jnp.arange(share, dtype=jnp.int32)
    row_valid = (row_ids < text_count[0]).astype(jnp.float32)[:, None]
    vmem = pl.BlockSpec(memory_space=pltpu.VMEM)
    chunks = width // WIDTH
    dma = pltpu.SemaphoreType.DMA
    video_out, text_out = pl.pallas_call(
        functools.partial(main_kernel, n),
        out_shape=(
            jax.ShapeDtypeStruct((tokens, width), jnp.bfloat16),
            jax.ShapeDtypeStruct((share, width), jnp.bfloat16),
        ),
        in_specs=[vmem] * 10,
        out_specs=(vmem, vmem),
        scratch_shapes=[
            pltpu.VMEM((4, 2, chunks, tokens, WIDTH), jnp.bfloat16),
            pltpu.VMEM((4, 8, tokens), jnp.float32),
            pltpu.VMEM((2, chunks, tokens, WIDTH), jnp.bfloat16),
            pltpu.VMEM((n, share, width // 2), jnp.bfloat16),
            pltpu.VMEM((n, share, 128), jnp.float32),
            pltpu.VMEM((n, share, width // 2), jnp.bfloat16),
            pltpu.VMEM((n, share, 128), jnp.float32),
            dma((4, 2, chunks)),
            dma((4, 2, chunks)),
            dma((4,)),
            dma((4,)),
            dma((2, chunks)),
            dma((2, chunks)),
            dma((2, chunks)),
            dma((2, n)),
            dma((2, n)),
        ],
        compiler_params=pltpu.CompilerParams(
            collective_id=0, has_side_effects=True, vmem_limit_bytes=56 * 1024 * 1024
        ),
    )(
        video_q, video_k, video_v, text_q, text_k, text_v, pick, own_bias, query_valid, row_valid
    )
    return (video_out, text_out)


def solution(mesh):
    return jax.shard_map(
        per_device,
        mesh=mesh,
        in_specs=(
            P(("groups", "tiles"), None),
            P(("groups", "tiles"), None),
            P(("groups", "tiles"), None),
            P("groups", None),
            P("groups", None),
            P("groups", None),
            P("tiles", None),
            P(("groups", "tiles")),
            P("groups"),
        ),
        out_specs=(P(("groups", "tiles"), None), P(("groups", "tiles"), None)),
        check_vma=False,
    )
```

```python
import functools
import math

import jax
import jax.numpy as jnp
from jax import lax
from jax.experimental import pallas as pl
from jax.experimental.pallas import tpu as pltpu
from jax.sharding import PartitionSpec as P

HEADS = 24
HD = 128
NR = 4
WIDTH = 256
LOG2E_SCALE = math.log2(math.e) / math.sqrt(HD)
MESH = pl.DeviceIdType.MESH
NT = (((1,), (1,)), ((), ()))


def main_kernel(
    n, q_ref, k_ref, v_ref, tq_ref, tk_ref, tv_ref, pick_ref, own_ref, qv_ref, tok_ref,
    out_ref, tout_ref,
    near, near_bias, relay, tnum, tstat, rnum, rstat,
    send_sem, recv_sem, bsend_sem, brecv_sem, fsend_sem, rsend_sem, rrecv_sem, tsend_sem, trecv_sem,
):
    group = lax.axis_index("groups")
    me = lax.axis_index("tiles")
    last = n // NR - 1
    chunks = q_ref.shape[1] // WIDTH
    per_chunk = WIDTH // HD
    tokens = q_ref.shape[0]
    half = tokens // 2
    share = tout_ref.shape[0]

    def at(offset):
        return lax.rem(me + offset + n, n)

    def time_of(index):
        return lax.div(lax.rem(index + n // 2 + NR + NR // 2, n), NR)

    row = lax.rem(me + n // 2 + NR + NR // 2, NR)
    time = time_of(me)
    side = lax.rem(me, 2)
    has = (time > 0, time < last, row > 0, row < NR - 1)
    offs = (-NR, NR, -1, 1)
    even = lax.rem(row, 2) == 0
    odd = lax.rem(row, 2) == 1
    quarter = lax.rem(me, 4)
    wrap_up = (quarter == 1) & (me < NR) & (time > 0)
    wrap_down = (quarter == 1) & (me >= n - NR) & (time < last)
    relay_up = (quarter == 3) & (me < NR) & (time_of(at(-2)) > 0)
    relay_down = (quarter == 3) & (me >= n - NR) & (time_of(at(-2)) < last)
    forward_down = (row == 1) & (time > 0)
    forward_up = (row == 2) & (time < last)

    barrier = pltpu.get_barrier_semaphore()

    def greet(i, _):
        pl.semaphore_signal(barrier, inc=1, device_id=(group, at(i)), device_id_type=MESH)
        return 0

    lax.fori_loop(1, n, greet, 0)
    pl.semaphore_wait(barrier, n - 1)

    def remote(source, target, sent, got, to):
        return pltpu.make_async_remote_copy(
            src_ref=source, dst_ref=target, send_sem=sent, recv_sem=got,
            device_id=(group, to), device_id_type=MESH,
        )

    def block(kv, c):
        cols = pl.ds(pl.multiple_of(c * WIDTH, WIDTH), WIDTH)
        return (k_ref, v_ref)[kv].at[:, cols]

    def bias_copy(d):
        return remote(own_ref, near_bias.at[d], bsend_sem.at[d], brecv_sem.at[d], at(-offs[d]))

    def direct(d, kv, c):
        return remote(
            block(kv, c), near.at[d, kv, c], send_sem.at[d, kv, c], recv_sem.at[d, kv, c], at(-offs[d])
        )

    def to_relay(d, kv, c):
        return remote(
            block(kv, c), relay.at[kv, c], send_sem.at[d, kv, c], rrecv_sem.at[kv, c], at(2)
        )

    def from_relay(d, kv, c):
        return remote(
            relay.at[kv, c], near.at[d, kv, c], rsend_sem.at[kv, c], recv_sem.at[d, kv, c],
            at(-2 - offs[d]),
        )

    def forward(d, kv, c):
        slot, to = (2, at(1 - NR)) if d == 0 else (3, at(NR - 1))
        return remote(
            near.at[d, kv, c], near.at[slot, kv, c], fsend_sem.at[kv, c], recv_sem.at[slot, kv, c], to
        )

    pair_sends = (((2, even), (0, 1)), ((3, odd), (0, 1)))
    far_sends = (
        ((0, (time < last) & jnp.logical_not(wrap_down)), (0, 1)),
        ((0, wrap_down), (1,)),
        ((1, (time > 0) & jnp.logical_not(wrap_up)), (0, 1)),
        ((2, (row == 1) & (time == last)), (0, 1)),
        ((3, (row == 2) & (time == 0)), (0, 1)),
    )
    relay_sends = (((0, wrap_down), (0,)), ((1, wrap_up), (0, 1)))
    onward = (((0, relay_down), (0,)), ((1, relay_up), (0, 1)))
    forwards = (((0, forward_down), (0, 1)), ((1, forward_up), (0, 1)))

    def each(table, make, act, c):
        for (d, when), kinds in table:
            @pl.when(when)
            def _(d=d, kinds=kinds):
                for kv in kinds:
                    act(make(d, kv, c))

    def start(copy):
        copy.start()

    def wait_send(copy):
        copy.wait_send()

    bias_sends = (has[1], has[0], has[3], has[2])
    for d in range(4):
        @pl.when(bias_sends[d])
        def _(d=d):
            bias_copy(d).start()

    def start_far(c, _):
        each(relay_sends, to_relay, start, c)
        each(far_sends, direct, start, c)

        def pass_on(d, kinds):
            for kv in kinds:
                pltpu.make_async_remote_copy(
                    src_ref=block(kv, c), dst_ref=relay.at[kv, c], send_sem=send_sem.at[d, kv, c],
                    recv_sem=rrecv_sem.at[kv, c], device_id=(group, at(2)), device_id_type=MESH,
                ).wait_recv()
                from_relay(d, kv, c).start()

        for (d, when), kinds in onward:
            @pl.when(when)
            def _(d=d, kinds=kinds):
                pass_on(d, kinds)
        return 0

    def start_pair(c, _):
        each(pair_sends, direct, start, c)
        return 0

    def missing(d):
        near_bias[d] = jnp.full(near_bias.shape[1:], -jnp.inf, jnp.float32)

        def clear(c, _):
            near[d, 0, c] = jnp.zeros(near.shape[3:], jnp.bfloat16)
            near[d, 1, c] = jnp.zeros(near.shape[3:], jnp.bfloat16)
            return 0

        lax.fori_loop(0, chunks, clear, 0)

    lax.fori_loop(0, 2, start_far, 0)
    lax.fori_loop(0, chunks, start_pair, 0)
    for d in range(4):
        @pl.when(jnp.logical_not(has[d]))
        def _(d=d):
            missing(d)

        @pl.when(has[d])
        def _(d=d):
            bias_copy(d).wait_recv()

    text_chunks = chunks // 2
    first = side * text_chunks
    lanes = lax.broadcasted_iota(jnp.int32, (share, 128), 1)

    def pair_arrived(c, _):
        for d, when in ((3, even), (2, odd)):
            @pl.when(when)
            def _(d=d):
                direct(d, 0, c).wait_recv()
                direct(d, 1, c).wait_recv()
        return 0

    lax.fori_loop(0, chunks, pair_arrived, 0)
    pair_slot = 3 - lax.rem(row, 2)
    tstat[...] = jnp.zeros_like(tstat)

    def text_part(j, _):
        c = first + j
        for h in range(per_chunk):
            cols = pl.ds(pl.multiple_of(c * WIDTH + h * HD, HD), HD)
            here = slice(h * HD, (h + 1) * HD)
            to = pl.ds(pl.multiple_of(j * WIDTH + h * HD, HD), HD)
            q = tq_ref[:, cols]
            s0 = lax.dot_general(q, k_ref[:, cols], NT, preferred_element_type=jnp.float32)
            s1 = lax.dot_general(
                q, near[pair_slot, 0, c, :, here], NT, preferred_element_type=jnp.float32
            )
            s0 = s0 + own_ref[0:1, :]
            s1 = s1 + near_bias[pair_slot, 0:1, :]
            top = jnp.max(jnp.maximum(s0, s1), axis=1, keepdims=True)
            p0 = jnp.exp2((s0 - top) * LOG2E_SCALE)
            p1 = jnp.exp2((s1 - top) * LOG2E_SCALE)
            total = jnp.sum(p0 + p1, axis=1, keepdims=True)
            num = None
            for p, value in ((p0, v_ref[:, cols]), (p1, near[pair_slot, 1, c, :, here])):
                wide = p * 65537.0
                high = wide - (wide - p)
                for part in (high, p - high):
                    term = jnp.dot(
                        part.astype(jnp.bfloat16), value, preferred_element_type=jnp.float32
                    )
                    num = term if num is None else num + term
            head = j * per_chunk + h
            for b in range(n):
                rows = slice(b * share, (b + 1) * share)
                tnum[b, :, to] = num[rows]
                stat = jnp.where(lanes == head, top[rows], tstat[b])
                tstat[b] = jnp.where(lanes == head + 64, total[rows], stat)
        return 0

    lax.fori_loop(0, text_chunks, text_part, 0)

    def text_copies(i, there, here):
        return (
            remote(tnum.at[there], rnum.at[here], tsend_sem.at[0, i], trecv_sem.at[0, i], there),
            remote(tstat.at[there], rstat.at[here], tsend_sem.at[1, i], trecv_sem.at[1, i], there),
        )

    def start_text(i, _):
        for copy in text_copies(i, at(i), me):
            copy.start()
        return 0

    lax.fori_loop(1, n, start_text, 0)
    rnum[me] = tnum[me]
    rstat[me] = tstat[me]
    lax.fori_loop(2, chunks, start_far, 0)

    waits = (
        (0, has[0]), (1, has[1]),
        (2, has[2] & even), (3, has[3] & odd),
    )

    def attend(c, _):
        for d, when in waits[:2]:
            @pl.when(when)
            def _(d=d):
                direct(d, 0, c).wait_recv()
                direct(d, 1, c).wait_recv()
        each(forwards, forward, start, c)
        for d, when in waits[2:]:
            @pl.when(when)
            def _(d=d):
                direct(d, 0, c).wait_recv()
                direct(d, 1, c).wait_recv()
        for h in range(WIDTH // HD):
            cols = pl.ds(pl.multiple_of(c * WIDTH + h * HD, HD), HD)
            here = slice(h * HD, (h + 1) * HD)
            q = q_ref[:, cols]
            scores = []
            for b in range(6):
                if b == 0:
                    key, extra = k_ref[:, cols], own_ref[0:1, :]
                elif b == 5:
                    key, extra = tk_ref[:, cols], None
                else:
                    key, extra = near[b - 1, 0, c, :, here], near_bias[b - 1, 0:1, :]
                s = lax.dot_general(q, key, NT, preferred_element_type=jnp.float32)
                parts = []
                for t in range(2):
                    bias = pick_ref[b, t:t + 1, :]
                    if extra is not None:
                        bias = bias + extra
                    parts.append(s[t * half:(t + 1) * half] + bias)
                scores.append(jnp.concatenate(parts, axis=0))
            top = functools.reduce(jnp.maximum, scores)
            top = jnp.max(top, axis=1, keepdims=True)
            total, num = None, None
            for b in range(6):
                p = jnp.exp2((scores[b] - top) * LOG2E_SCALE)
                total = p if total is None else total + p
                if b == 0:
                    value = v_ref[:, cols]
                elif b == 5:
                    value = tv_ref[:, cols]
                else:
                    value = near[b - 1, 1, c, :, here]
                term = jnp.dot(p.astype(jnp.bfloat16), value, preferred_element_type=jnp.float32)
                num = term if num is None else num + term
            total = jnp.sum(total, axis=1, keepdims=True)
            result = jnp.where(qv_ref[...] > 0, num / total, 0.0)
            out_ref[:, cols] = result.astype(jnp.bfloat16)
        return 0

    lax.fori_loop(0, chunks, attend, 0)

    def finish(c, _):
        each(pair_sends, direct, wait_send, c)
        each(far_sends, direct, wait_send, c)
        each(relay_sends, to_relay, wait_send, c)
        each(onward, from_relay, wait_send, c)
        each(forwards, forward, wait_send, c)
        return 0

    def text_arrived(i, _):
        for copy in text_copies(i, at(n - i), at(n - i)):
            copy.wait_recv()
        for copy in text_copies(i, at(i), me):
            copy.wait_send()
        return 0

    lax.fori_loop(1, n, text_arrived, 0)

    heads = tnum.shape[2] // HD
    for e in range(2):
        top = lax.fori_loop(
            1, n // 2, lambda i, m: jnp.maximum(m, rstat[2 * i + e]), rstat[e]
        )

        def add(i, carry):
            den, nums = carry
            stat = rstat[2 * i + e]
            scale = jnp.exp2((stat - top) * LOG2E_SCALE)
            den = den + scale * jnp.roll(stat, 64, axis=1)
            nums = tuple(
                nums[j]
                + rnum[2 * i + e, :, j * HD:(j + 1) * HD].astype(jnp.float32) * scale[:, j:j + 1]
                for j in range(heads)
            )
            return den, nums

        zeros = jnp.zeros((share, HD), jnp.float32)
        den, nums = lax.fori_loop(0, n // 2, add, (zeros, (zeros,) * heads))
        for j in range(heads):
            result = jnp.where(tok_ref[...] > 0, nums[j] / den[:, j:j + 1], 0.0)
            at_head = (e * heads + j) * HD
            tout_ref[:, at_head:at_head + HD] = result.astype(jnp.bfloat16)

    for d in range(4):
        @pl.when(bias_sends[d])
        def _(d=d):
            bias_copy(d).wait_send()
    lax.fori_loop(0, chunks, finish, 0)


def per_device(video_q, video_k, video_v, text_q, text_k, text_v, window, counts, text_count):
    n = lax.axis_size("tiles")
    position = lax.axis_index("tiles")
    tiles = counts.shape[0]
    tokens, width = video_q.shape
    tok = tokens // tiles
    text = text_q.shape[0]
    share = text // n
    slots = jnp.arange(tok, dtype=jnp.int32)
    valid = (slots[None, :] < counts[:, None]).reshape(-1)
    own_bias = jnp.broadcast_to(jnp.where(valid, 0.0, -jnp.inf)[None, :], (8, tokens))
    codes = jnp.concatenate([jnp.ones((tiles, 1), jnp.int32), window + (window >= 1)], axis=1)
    column = jnp.arange(tiles, dtype=jnp.int32)[:, None] + codes % 3 - 1
    block_ids = jnp.arange(5, dtype=jnp.int32)[:, None, None, None]
    column_ids = jnp.arange(tiles, dtype=jnp.int32)[None, None, :, None]
    hit = jnp.any(
        (codes[None, :, None, :] // 3 == block_ids) & (column[None, :, None, :] == column_ids),
        axis=-1,
    )
    pick = jnp.broadcast_to(hit[..., None], (5, tiles, tiles, tok)).reshape(5, tiles, tokens)
    text_ok = jnp.arange(text, dtype=jnp.int32) < text_count[0]
    text_pick = jnp.broadcast_to(text_ok[None, None, :], (1, tiles, text))
    pick = jnp.where(jnp.concatenate([pick, text_pick], axis=0), 0.0, -jnp.inf)
    pick = jnp.pad(pick, ((0, 0), (0, 8 - tiles), (0, 0)))
    query_valid = valid.astype(jnp.float32)[:, None]

    row_ids = position * share + jnp.arange(share, dtype=jnp.int32)
    row_valid = (row_ids < text_count[0]).astype(jnp.float32)[:, None]
    vmem = pl.BlockSpec(memory_space=pltpu.VMEM)
    chunks = width // WIDTH
    dma = pltpu.SemaphoreType.DMA
    video_out, text_out = pl.pallas_call(
        functools.partial(main_kernel, n),
        out_shape=(
            jax.ShapeDtypeStruct((tokens, width), jnp.bfloat16),
            jax.ShapeDtypeStruct((share, width), jnp.bfloat16),
        ),
        in_specs=[vmem] * 10,
        out_specs=(vmem, vmem),
        scratch_shapes=[
            pltpu.VMEM((4, 2, chunks, tokens, WIDTH), jnp.bfloat16),
            pltpu.VMEM((4, 8, tokens), jnp.float32),
            pltpu.VMEM((2, chunks, tokens, WIDTH), jnp.bfloat16),
            pltpu.VMEM((n, share, width // 2), jnp.float32),
            pltpu.VMEM((n, share, 128), jnp.float32),
            pltpu.VMEM((n, share, width // 2), jnp.float32),
            pltpu.VMEM((n, share, 128), jnp.float32),
            dma((4, 2, chunks)),
            dma((4, 2, chunks)),
            dma((4,)),
            dma((4,)),
            dma((2, chunks)),
            dma((2, chunks)),
            dma((2, chunks)),
            dma((2, n)),
            dma((2, n)),
        ],
        compiler_params=pltpu.CompilerParams(
            collective_id=0, has_side_effects=True, vmem_limit_bytes=56 * 1024 * 1024
        ),
    )(
        video_q, video_k, video_v, text_q, text_k, text_v, pick, own_bias, query_valid, row_valid
    )
    return (video_out, text_out)


def solution(mesh):
    return jax.shard_map(
        per_device,
        mesh=mesh,
        in_specs=(
            P(("groups", "tiles"), None),
            P(("groups", "tiles"), None),
            P(("groups", "tiles"), None),
            P("groups", None),
            P("groups", None),
            P("groups", None),
            P("tiles", None),
            P(("groups", "tiles")),
            P("groups"),
        ),
        out_specs=(P(("groups", "tiles"), None), P(("groups", "tiles"), None)),
        check_vma=False,
    )
```
